32 devices in a mesh: ka: 4 (over x, core), fit: 8 (over z, y).
Axes of the slice: x: 2, y: 2, z: 4, core: 2. Of those that a mesh axis runs over, the one named last changes fastest.
Arguments:
- integrals: bfloat16 [3, 4, 8, 48, 64, 128], P(None, 'ka', 'fit'), may hold values from -0.3125 to 0.3125
- block_lists: int32 [3, 4, 8, 2, 48], P(None, 'ka', 'fit'), may hold values from 0 to 15, as said below
- coeff: bfloat16 [4, 2, 1024, 256], P('ka', None, 'fit'), may hold values from -6 to 6
- match: int32 [3, 4], replicated, may hold values from 0 to 3, each once within a row
- ex_blocks: int32 [4, 2, 64], P('ka'), may hold values from 0 to 15, as said below
Outputs:
- exchange: float32 [4, 4096, 128], P('ka', 'fit')
The draws below stay inside these ranges and needn't reach their ends.
Inputs may be any that keep to these rules, and one draw needn't show every extreme that they name: `block_lists`: each integral matrix lists 48 distinct blocks; each entry is a block index below 16, row first then column. `ex_blocks`: each k-point lists 64 distinct blocks, none on the diagonal (row block differs from column block).
All inputs are finite; a program needn't handle non-finite values.
Results may differ from the reference program's by a relative error of at most 0.0036.
Values may be sent and summed in bfloat16 or wider, within the bound.
No kernel may reach another device: no remote copies, remote signals or barrier semaphores. Data moves between devices by JAX's collectives and lax.ppermute only.
A program may use at most 128 MiB of HBM per device.

```python
import jax
import jax.numpy as jnp
from jax import lax

NAO = 1024
NOCC = 256
EDGE = 64
NQ = 3
NBLK = 48
EXB = 64
NK = 4
NAUX = 8
NB = 16


def draw_block_lists(key, part):
    keys = jax.random.split(jax.random.fold_in(key, 11), NQ * NK * NAUX)
    ids = jax.vmap(lambda one: jax.random.permutation(one, NB * NB)[:NBLK])(keys)
    lists = jnp.stack([ids // NB, ids % NB], axis=1)
    return lists.reshape(NQ, NK, NAUX, 2, NBLK).astype(jnp.int32)


def draw_ex_blocks(key, part):
    keys = jax.random.split(jax.random.fold_in(key, 23), NK)
    ids = jax.vmap(lambda one: jax.random.permutation(one, NB * (NB - 1))[:EXB])(keys)
    rowblk = ids // (NB - 1)
    other = ids % (NB - 1)
    colblk = other + (other >= rowblk).astype(jnp.int32)
    return jnp.stack([rowblk, colblk], axis=1).astype(jnp.int32)


def level_of(stream_key, extent, cuts, least, high):
    def one(dim, shards_of):
        steps = jax.random.uniform(jax.random.fold_in(jax.random.fold_in(stream_key, 6), dim), (shards_of,), jnp.float32, least / len(cuts), high / len(cuts))
        return jnp.repeat(jnp.exp(steps), extent[dim] // shards_of).reshape((-1,) + (1,) * (len(extent) - dim - 1))

    gain = one(*cuts[0])
    for cut in cuts[1:]:
        gain = gain * one(*cut)
    return gain


def gaussian(rng, extent, scale, bound, cuts=(), kind=jnp.bfloat16):
    array = scale * jax.random.normal(rng, extent, jnp.float32)
    if cuts:
        array = array * level_of(rng, extent, cuts, -0.22, 0.18)
    return jnp.clip(array, -bound, bound).astype(kind)


def setup_inputs(seed: int = 0) -> dict:
    key_list = jax.random.split(jax.random.key(seed), 6)
    return {
        "integrals": gaussian(key_list[0], (NQ, NK, NAUX, NBLK, EDGE, 2 * EDGE), (8 * NBLK) ** -0.5, 0.3125, ((1, 4), (2, 8))),
        "block_lists": draw_block_lists(jax.random.fold_in(key_list[5], 71), 0),
        "coeff": gaussian(key_list[2], (NK, 2, NAO, NOCC), 1.0, 6.0, ((0, 4), (2, 8))),
        "match": jax.vmap(lambda own: jax.random.permutation(own, NK))(jax.random.split(key_list[3], NQ)).reshape((NQ, NK)).astype(jnp.int32),
        "ex_blocks": draw_ex_blocks(jax.random.fold_in(key_list[5], 71), 0),
    }


def block_operands(coeff_one, edge):
    nblocks = coeff_one.shape[1] // edge
    real = coeff_one[0].reshape(nblocks, edge, -1)
    imag = coeff_one[1].reshape(nblocks, edge, -1)
    upper = jnp.concatenate([real, imag], axis=2)
    lower = jnp.concatenate([-imag, real], axis=2)
    return jnp.concatenate([upper, lower], axis=1)


def half_transform(lmat, lists, operands):
    nblocks = operands.shape[0]
    picked = jnp.take(operands, lists[1], axis=0).astype(jnp.float32)
    prods = jnp.einsum("bmi,bij->bmj", lmat.astype(jnp.float32), picked, precision=lax.Precision.HIGHEST)
    onehot = (lists[0][None, :] == jnp.arange(nblocks, dtype=jnp.int32)[:, None]).astype(jnp.float32)
    rows = jnp.einsum("rb,bmj->rmj", onehot, prods, precision=lax.Precision.HIGHEST)
    return rows.astype(jnp.bfloat16)


def exchange_blocks(xmat, listed):
    occ = xmat.shape[2] // 2
    left = jnp.take(xmat, listed[0], axis=0).astype(jnp.float32)
    right = jnp.take(xmat, listed[1], axis=0).astype(jnp.float32)
    swapped = jnp.concatenate([left[:, :, occ:], -left[:, :, :occ]], axis=2)
    kreal = jnp.einsum("emj,enj->emn", left, right, precision=lax.Precision.HIGHEST)
    kimag = jnp.einsum("emj,enj->emn", swapped, right, precision=lax.Precision.HIGHEST)
    return jnp.concatenate([kreal, kimag], axis=2)


def reference(integrals, block_lists, coeff, match, ex_blocks):
    edge = integrals.shape[4]
    operands_all = jnp.stack([block_operands(coeff[k], edge) for k in range(NK)])
    factor = -((NQ * NAUX * NOCC) ** -0.5)
    outs = []
    for kpt in range(NK):
        def step(index, acc):
            qq = index // NAUX
            pp = index % NAUX
            partner = match[qq, kpt]
            operands = operands_all[partner]
            xmat = half_transform(integrals[qq, kpt, pp], block_lists[qq, kpt, pp], operands)
            xmat = lax.optimization_barrier(xmat)
            return acc + exchange_blocks(xmat, ex_blocks[kpt])
        start = jnp.zeros((EXB, edge, 2 * edge), jnp.float32)
        acc = lax.fori_loop(0, NQ * NAUX, step, start)
        outs.append((acc * factor).reshape(EXB * edge, 2 * edge))
    return jnp.stack(outs)
```

```python
import functools

import jax
import jax.numpy as jnp
from jax import lax
from jax.experimental import pallas as pl
from jax.experimental.pallas import tpu as pltpu
from jax.sharding import PartitionSpec as P

AXES = ("ka", "fit")


def bits_of(size):
    return [1 << b for b in range(size.bit_length() - 1)]


def gather_pieces(shard, nka, nfit):
    def swap(arr, dka, dfit):
        perm = [
            (k * nfit + f, (k ^ dka) * nfit + (f ^ dfit))
            for k in range(nka)
            for f in range(nfit)
        ]
        return lax.ppermute(arr, AXES, perm)

    core, xbit = 1, nka // 2
    fit_bits = bits_of(nfit)
    ybit, wbit = fit_bits[0], fit_bits[1]
    got = {}

    def send(key, dka, dfit):
        kind, ka, fit = key
        got[(kind, ka ^ dka, fit ^ dfit)] = swap(got[key], dka, dfit)

    x, y, w = (xbit, 0), (0, ybit), (0, wbit)
    a, b = ("near", 0, 0), ("far", 0, 0)

    def at(key, *steps):
        kind, ka, fit = key
        for dka, dfit in steps:
            ka, fit = ka ^ dka, fit ^ dfit
        return (kind, ka, fit)

    got[a] = shard
    stack = shard
    offsets = [0]
    for bit in fit_bits[2:]:
        stack = jnp.concatenate([stack, swap(stack, 0, bit)], axis=0) if bit != fit_bits[-1] or len(fit_bits) > 3 else None
        offsets = offsets + [o ^ bit for o in offsets]
    if stack is None:
        got[b] = swap(shard, 0, fit_bits[2])
    else:
        got[b] = stack[1:]
    send(a, *x)
    send(a, *y)
    send(a, *w)
    send(b, *x)
    send(at(a, w), *x)
    send(b, *y)
    send(at(a, x), *y)
    send(b, *w)
    send(at(a, y), *w)
    send(at(a, y, w), *x)
    send(at(b, y), *x)
    send(at(b, w), *y)
    send(at(b, x), *w)
    send(at(b, y, w), *x)
    for key in list(got):
        send(key, core, 0)
    return got, offsets[1:]


def exchange_kernel(
    keys, far, nq, nblk, nexch, edge, occ, nbl, match_ref, lists_ref, ex_ref, lmat_ref, *refs
):
    pieces = refs[: len(keys)]
    out_ref, ops_ref, sums_ref, x_ref = refs[len(keys) :]
    ka, fit = lax.axis_index("ka"), lax.axis_index("fit")
    rows = pieces[0].shape[2]
    sub = min(rows, edge)

    def one_q(qq, carry):
        want = lax.bitwise_xor(match_ref[qq, ka], ka)

        for dka in sorted({key[1] for key in keys}):

            @pl.when(want == dka)
            def _():
                for key, piece in zip(keys, pieces):
                    if key[1] != dka:
                        continue
                    offs = [key[2]] if key[0] == "near" else [key[2] ^ o for o in far]
                    for index, off in enumerate(offs):
                        owner = lax.bitwise_xor(fit, off)
                        for part in range(rows // sub):
                            row = owner * rows + part * sub
                            dst = (row // edge) * (2 * edge) + lax.rem(row, edge)
                            dst = pl.multiple_of(dst, sub)
                            real = piece[index, 0, part * sub : (part + 1) * sub, :]
                            imag = piece[index, 1, part * sub : (part + 1) * sub, :]
                            ops_ref[pl.ds(dst, sub), :occ] = real
                            ops_ref[pl.ds(dst, sub), occ:] = imag
                            low = pl.multiple_of(dst + edge, sub)
                            ops_ref[pl.ds(low, sub), :occ] = -imag
                            ops_ref[pl.ds(low, sub), occ:] = real

        sums_ref[...] = jnp.zeros_like(sums_ref)

        def one_block(n, c):
            rb = pl.multiple_of(lists_ref[qq, 0, 0, 0, n] * edge, edge)
            cb = pl.multiple_of(lists_ref[qq, 0, 0, 1, n] * (2 * edge), 2 * edge)
            sums_ref[pl.ds(rb, edge), :] += jnp.dot(
                lmat_ref[qq, 0, 0, n],
                ops_ref[pl.ds(cb, 2 * edge), :],
                preferred_element_type=jnp.float32,
            )
            return c

        lax.fori_loop(0, nblk, one_block, 0, unroll=4)

        for rb in range(nbl):
            x = sums_ref[rb * edge : (rb + 1) * edge, :].astype(jnp.bfloat16)
            x_ref[qq, rb, :edge, :] = x
            x_ref[qq, rb, edge:, :occ] = -x[:, occ:]
            x_ref[qq, rb, edge:, occ:] = x[:, :occ]
        return carry

    lax.fori_loop(0, nq, one_q, 0)

    def one_pair(e, c):
        left, right = ex_ref[0, 0, e], ex_ref[0, 1, e]
        acc = None
        for qq in range(nq):
            term = lax.dot_general(
                x_ref[qq, left, :edge, :],
                x_ref[qq, right],
                (((1,), (1,)), ((), ())),
                preferred_element_type=jnp.float32,
            )
            acc = term if acc is None else acc + term
        out_ref[pl.ds(pl.multiple_of(e * edge, edge), edge), :] = acc.astype(out_ref.dtype)
        return c

    lax.fori_loop(0, nexch, one_pair, 0, unroll=4)


def on_device(nka, nfit, integrals, block_lists, coeff, match, ex_blocks):
    nq, _, _, nblk, edge, _ = integrals.shape
    occ = coeff.shape[3]
    nexch = ex_blocks.shape[2]
    nbl = nfit * coeff.shape[2] // edge
    got, far = gather_pieces(coeff, nka, nfit)
    keys = sorted(got)
    vmem = pl.BlockSpec(memory_space=pltpu.VMEM)
    smem = pl.BlockSpec(memory_space=pltpu.SMEM)
    partial = pl.pallas_call(
        functools.partial(exchange_kernel, keys, far, nq, nblk, nexch, edge, occ, nbl),
        out_shape=jax.ShapeDtypeStruct((nexch * edge, 2 * edge), jnp.bfloat16),
        in_specs=[smem, smem, smem, vmem] + [vmem] * len(keys),
        out_specs=vmem,
        scratch_shapes=[
            pltpu.VMEM((nbl * 2 * edge, 2 * occ), jnp.bfloat16),
            pltpu.VMEM((nbl * edge, 2 * occ), jnp.float32),
            pltpu.VMEM((nq, nbl, 2 * edge, 2 * occ), jnp.bfloat16),
        ],
        compiler_params=pltpu.CompilerParams(vmem_limit_bytes=48 * 1024 * 1024),
    )(match, block_lists, ex_blocks, integrals, *[got[key] for key in keys])
    spread = lax.all_to_all(partial, "fit", 0, 0, tiled=True)
    factor = -((nq * nfit * occ) ** (-0.5))
    parts = spread.reshape(nfit, nexch * edge // nfit, 2 * edge).astype(jnp.float32)
    return (jnp.sum(parts, axis=0) * factor)[None]


def solution(mesh):
    nka, nfit = mesh.shape["ka"], mesh.shape["fit"]
    return jax.shard_map(
        functools.partial(on_device, nka, nfit),
        mesh=mesh,
        in_specs=(
            P(None, "ka", "fit", None, None, None),
            P(None, "ka", "fit", None, None),
            P("ka", None, "fit", None),
            P(),
            P("ka", None, None),
        ),
        out_specs=P("ka", "fit", None),
        check_vma=False,
    )
```

```python
import functools

import jax
import jax.numpy as jnp
from jax import lax
from jax.experimental import pallas as pl
from jax.experimental.pallas import tpu as pltpu
from jax.sharding import PartitionSpec as P

AXES = ("ka", "fit")


def bits_of(size):
    return [1 << b for b in range(size.bit_length() - 1)]


def gather_pieces(shard, nka, nfit):
    def swap(arr, dka, dfit):
        perm = [
            (k * nfit + f, (k ^ dka) * nfit + (f ^ dfit))
            for k in range(nka)
            for f in range(nfit)
        ]
        return lax.ppermute(arr, AXES, perm)

    core, xbit = 1, nka // 2
    fit_bits = bits_of(nfit)
    ybit, wbit = fit_bits[0], fit_bits[1]
    got = {}

    def send(key, dka, dfit):
        kind, ka, fit = key
        got[(kind, ka ^ dka, fit ^ dfit)] = swap(got[key], dka, dfit)

    x, y, w = (xbit, 0), (0, ybit), (0, wbit)
    a, b = ("near", 0, 0), ("far", 0, 0)

    def at(key, *steps):
        kind, ka, fit = key
        for dka, dfit in steps:
            ka, fit = ka ^ dka, fit ^ dfit
        return (kind, ka, fit)

    got[a] = shard
    stack = shard
    offsets = [0]
    for bit in fit_bits[2:]:
        stack = jnp.concatenate([stack, swap(stack, 0, bit)], axis=0) if bit != fit_bits[-1] or len(fit_bits) > 3 else None
        offsets = offsets + [o ^ bit for o in offsets]
    if stack is None:
        got[b] = swap(shard, 0, fit_bits[2])
    else:
        got[b] = stack[1:]
    send(a, *x)
    send(a, *y)
    send(a, *w)
    send(b, *x)
    send(at(a, w), *x)
    send(b, *y)
    send(at(a, x), *y)
    send(b, *w)
    send(at(a, y), *w)
    send(at(a, y, w), *x)
    send(at(b, y), *x)
    send(at(b, w), *y)
    send(at(b, x), *w)
    send(at(b, y, w), *x)
    for key in list(got):
        send(key, core, 0)
    return got, offsets[1:]


def exchange_units(order, second, unit, edge, x_ref, turned_ref, ex_ref, out_ref):
    fit = lax.axis_index("fit")
    half = out_ref.shape[1]
    steps = half // unit
    for slot, off in enumerate(order):
        owner = lax.bitwise_xor(fit, off)
        for step in range(steps):
            row = owner * (2 * half) + second * half + step * unit
            e = row // edge
            lb, rb = ex_ref[0, 0, e], ex_ref[0, 1, e]
            lo = pl.multiple_of(lax.rem(row, edge), unit)
            out_ref[slot, step * unit : (step + 1) * unit, :] = jnp.dot(
                x_ref[lb, pl.ds(lo, unit), :],
                turned_ref[rb],
                preferred_element_type=jnp.float32,
            ).astype(out_ref.dtype)


def half_kernel(
    keys, far, orders, nq, nblk, edge, occ, nbl, match_ref, lists_ref, ex_ref, lmat_ref, *refs
):
    pieces = refs[: len(keys)]
    first_ref, second_ref, x_ref, turned_ref, l_ref, ops_ref, sums_ref, sems = refs[len(keys) :]
    ka, fit = lax.axis_index("ka"), lax.axis_index("fit")
    rows = pieces[0].shape[2]
    sub = min(rows, edge)
    copies = [
        pltpu.make_async_copy(lmat_ref.at[qq, 0, 0], l_ref.at[qq], sems.at[qq]) for qq in range(nq)
    ]
    for copy in copies:
        copy.start()

    for qq in range(nq):
        want = lax.bitwise_xor(match_ref[qq, ka], ka)

        for dka in sorted({key[1] for key in keys}):

            @pl.when(want == dka)
            def _():
                for key, piece in zip(keys, pieces):
                    if key[1] != dka:
                        continue
                    offs = [key[2]] if key[0] == "near" else [key[2] ^ o for o in far]
                    for index, off in enumerate(offs):
                        owner = lax.bitwise_xor(fit, off)
                        for part in range(rows // sub):
                            row = owner * rows + part * sub
                            dst = (row // edge) * (2 * edge) + lax.rem(row, edge)
                            dst = pl.multiple_of(dst, sub)
                            real = piece[index, 0, part * sub : (part + 1) * sub, :]
                            imag = piece[index, 1, part * sub : (part + 1) * sub, :]
                            ops_ref[pl.ds(dst, sub), :occ] = real
                            ops_ref[pl.ds(dst, sub), occ:] = imag
                            low = pl.multiple_of(dst + edge, sub)
                            ops_ref[pl.ds(low, sub), :occ] = -imag
                            ops_ref[pl.ds(low, sub), occ:] = real

        sums_ref[...] = jnp.zeros_like(sums_ref)
        copies[qq].wait()

        def one_block(n, c):
            rb = pl.multiple_of(lists_ref[qq, 0, 0, 0, n] * edge, edge)
            cb = pl.multiple_of(lists_ref[qq, 0, 0, 1, n] * (2 * edge), 2 * edge)
            sums_ref[pl.ds(rb, edge), :] += jnp.dot(
                l_ref[qq, n],
                ops_ref[pl.ds(cb, 2 * edge), :],
                preferred_element_type=jnp.float32,
            )
            return c

        lax.fori_loop(0, nblk, one_block, 0, unroll=16)

        def one_row(rb, c):
            x = sums_ref[pl.ds(pl.multiple_of(rb * edge, edge), edge), :].astype(jnp.bfloat16)
            x_ref[rb, :, qq * 2 * occ : (qq + 1) * 2 * occ] = x
            low = jnp.concatenate([-x[:, occ:], x[:, :occ]], axis=1)
            turned_ref[rb, qq * 2 * occ : (qq + 1) * 2 * occ, :] = jnp.concatenate([x, low], axis=0).T
            return c

        lax.fori_loop(0, nbl, one_row, 0, unroll=4)

    unit = min(edge, first_ref.shape[1])
    exchange_units(orders[0], 0, unit, edge, x_ref, turned_ref, ex_ref, first_ref)
    exchange_units(orders[1], 1, unit, edge, x_ref, turned_ref, ex_ref, second_ref)


def rest_kernel(orders, edge, ex_ref, x_ref, turned_ref, first_ref, second_ref):
    unit = min(edge, first_ref.shape[1])
    exchange_units(orders[0], 0, unit, edge, x_ref, turned_ref, ex_ref, first_ref)
    exchange_units(orders[1], 1, unit, edge, x_ref, turned_ref, ex_ref, second_ref)


def on_device(nka, nfit, integrals, block_lists, coeff, match, ex_blocks):
    nq, _, _, nblk, edge, _ = integrals.shape
    occ = coeff.shape[3]
    nexch = ex_blocks.shape[2]
    nbl = nfit * coeff.shape[2] // edge
    got, far = gather_pieces(coeff, nka, nfit)
    keys = sorted(got)
    vmem = pl.BlockSpec(memory_space=pltpu.VMEM)
    smem = pl.BlockSpec(memory_space=pltpu.SMEM)
    hbm = pl.BlockSpec(memory_space=pl.ANY)

    bits = bits_of(nfit)
    ybit, wbit, rest = bits[0], bits[1], bits[2:][::-1]
    far_offs = [0]
    for bit in rest[::-1]:
        far_offs = far_offs + [o ^ bit for o in far_offs]
    keep_a = far_offs + [o ^ wbit for o in far_offs]
    keep_b = far_offs + [o ^ ybit for o in far_offs]
    send_a = [o ^ ybit for o in keep_a]
    send_b = [o ^ wbit for o in keep_b]
    half = nexch * edge // nfit // 2
    count = len(keep_a)
    params = pltpu.CompilerParams(vmem_limit_bytes=28 * 1024 * 1024)

    def outs(dtype):
        return [jax.ShapeDtypeStruct((count, half, 2 * edge), dtype)] * 2

    xshape = (nbl, edge, nq * 2 * occ)
    tshape = (nbl, nq * 2 * occ, 2 * edge)
    out_a, out_b, xmat, turned = pl.pallas_call(
        functools.partial(
            half_kernel, keys, far, (send_a, send_b), nq, nblk, edge, occ, nbl
        ),
        out_shape=outs(jnp.bfloat16)
        + [jax.ShapeDtypeStruct(xshape, jnp.bfloat16), jax.ShapeDtypeStruct(tshape, jnp.bfloat16)],
        in_specs=[smem, smem, smem, hbm] + [vmem] * len(keys),
        out_specs=[vmem] * 4,
        scratch_shapes=[
            pltpu.VMEM((nq, nblk, edge, 2 * edge), jnp.bfloat16),
            pltpu.VMEM((nbl * 2 * edge, 2 * occ), jnp.bfloat16),
            pltpu.VMEM((nbl * edge, 2 * occ), jnp.float32),
            pltpu.SemaphoreType.DMA((nq,)),
        ],
        compiler_params=params,
    )(match, block_lists, ex_blocks, integrals, *[got[key] for key in keys])
    own_a, own_b = pl.pallas_call(
        functools.partial(rest_kernel, (keep_a, keep_b), edge),
        out_shape=outs(jnp.float32),
        in_specs=[smem, vmem, vmem],
        out_specs=[vmem] * 2,
        compiler_params=params,
        cost_estimate=pl.CostEstimate(
            flops=nexch * edge * edge * 2 * nq * 2 * occ, bytes_accessed=1 << 23, transcendentals=0
        ),
    )(ex_blocks, xmat, turned)

    def swap(arr, dfit):
        return lax.ppermute(arr, "fit", [(f, f ^ dfit) for f in range(nfit)])

    def down(arr):
        return arr.astype(jnp.bfloat16)

    def up(arr):
        return arr.astype(jnp.float32)

    n = count // 2
    got_a, got_b = swap(out_a, ybit), swap(out_b, wbit)
    sum_a = own_a + up(got_a)
    got_a = swap(down(sum_a[n:]), wbit)
    sum_b = own_b + up(got_b)
    got_b = swap(down(sum_b[n:]), ybit)
    both = jnp.concatenate([sum_a[:n] + up(got_a), sum_b[:n] + up(got_b)], axis=1)
    for bit in rest:
        n = n // 2
        both = both[:n] + up(swap(down(both[n:]), bit))
    factor = -((nq * nfit * occ) ** (-0.5))
    return both * factor


def solution(mesh):
    nka, nfit = mesh.shape["ka"], mesh.shape["fit"]
    return jax.shard_map(
        functools.partial(on_device, nka, nfit),
        mesh=mesh,
        in_specs=(
            P(None, "ka", "fit", None, None, None),
            P(None, "ka", "fit", None, None),
            P("ka", None, "fit", None),
            P(),
            P("ka", None, None),
        ),
        out_specs=P("ka", "fit", None),
        check_vma=False,
    )
```

```python
import functools

import jax
import jax.numpy as jnp
from jax import lax
from jax.experimental import pallas as pl
from jax.experimental.pallas import tpu as pltpu
from jax.sharding import PartitionSpec as P

AXES = ("ka", "fit")
TILE = 16


def bits_of(size):
    return [1 << b for b in range(size.bit_length() - 1)]


def near_dims(nka, nfit):
    low, second = bits_of(nfit)[:2]
    return (nka // 2, 0), (0, low), (0, second)


def gather_orders(nka, nfit):
    x, y, w = near_dims(nka, nfit)
    return ((x, y, w), (y, w, x)), ((w, x, y), (w, x, y))


def swap_by(arr, nka, nfit, by_core):
    perm = []
    for k in range(nka):
        dka, dfit = by_core[k & 1]
        for f in range(nfit):
            perm.append((k * nfit + f, (k ^ dka) * nfit + (f ^ dfit)))
    return lax.ppermute(arr, AXES, perm)


def far_offsets(nfit):
    offsets = [0]
    for bit in bits_of(nfit)[2:]:
        offsets = offsets + [o ^ bit for o in offsets]
    return offsets


def split_row(rows):
    return (2 * rows // 3 + TILE // 2) // TILE * TILE


def gather_shards(shard, nka, nfit):
    stack = shard.reshape(-1, shard.shape[-1])
    for bit in bits_of(nfit)[2:]:
        stack = jnp.concatenate([stack, swap_by(stack, nka, nfit, [(0, bit)] * 2)], axis=0)
    cut = split_row(stack.shape[0])
    parts = [stack[:cut], stack[cut:]]
    orders = gather_orders(nka, nfit)
    for step in range(3):
        fresh = [
            swap_by(part, nka, nfit, [order[core][step] for core in range(2)])
            for part, order in zip(parts, orders)
        ]
        if step < 2:
            parts = [jnp.concatenate(pair, axis=0) for pair in zip(parts, fresh)]
    held = [arr for pair in zip(parts, fresh) for arr in pair]
    return held + [swap_by(arr, nka, nfit, [(1, 0)] * 2) for arr in held]


def exchange_units(owner_of, unit, edge, x_ref, turned_ref, ex_ref, out_ref):
    count, rows, _ = out_ref.shape
    for slot in range(count):
        for step in range(rows // unit):
            row = owner_of(slot) * rows + step * unit
            e = row // edge
            lb, rb = ex_ref[0, 0, e], ex_ref[0, 1, e]
            lo = pl.multiple_of(lax.rem(row, edge), unit)
            out_ref[slot, step * unit : (step + 1) * unit, :] = jnp.dot(
                x_ref[lb, pl.ds(lo, unit), :],
                turned_ref[rb],
                preferred_element_type=jnp.float32,
            ).astype(out_ref.dtype)


def scatter_owner(keep, nfit):
    low, second = bits_of(nfit)[:2]
    offs = far_offsets(nfit)
    core, fit = lax.rem(lax.axis_index("ka"), 2), lax.axis_index("fit")
    first = jnp.where(core == 0, low, second)
    other = low + second - first

    def owner(slot):
        off = offs[slot % len(offs)]
        owner = lax.bitwise_xor(fit, off)
        if slot >= len(offs):
            owner = lax.bitwise_xor(owner, other)
        return owner if keep else lax.bitwise_xor(owner, first)

    return owner


def half_kernel(
    nka, nfit, nq, nblk, edge, occ, nbl, rows, match_hbm, lists_hbm, ex_hbm, lmat_ref, *refs
):
    held = refs[:8]
    out_ref, x_ref, turned_ref = refs[8:11]
    match_ref, lists_ref, ex_ref, l_ref, ops_ref, sums_ref, sems, small = refs[11:]
    ka, fit = lax.axis_index("ka"), lax.axis_index("fit")
    core = lax.rem(ka, 2)
    sub = min(rows, edge)
    loads = [
        pltpu.make_async_copy(src, dst, small.at[i])
        for i, (src, dst) in enumerate(
            [(match_hbm, match_ref), (lists_hbm, lists_ref), (ex_hbm, ex_ref)]
        )
    ]
    copies = [
        pltpu.make_async_copy(lmat_ref.at[qq, 0, 0], l_ref.at[qq], sems.at[qq]) for qq in range(nq)
    ]
    for copy in loads + copies:
        copy.start()
    for copy in loads:
        copy.wait()

    far = far_offsets(nfit)
    orders = gather_orders(nka, nfit)
    total = len(far) * 2 * rows
    cut = split_row(total)
    spans = [(0, cut), (cut, total)]

    def place(ref, base, span, owner):
        lo, hi = span
        row = lo
        while row < hi:
            piece, rest = divmod(row, 2 * rows)
            part, inner = divmod(rest, rows)
            size = min(hi - row, sub - inner % sub)
            start = lax.bitwise_xor(owner, far[piece]) * rows + inner
            dst = (start // edge) * (2 * edge) + lax.rem(start, edge)
            dst = pl.multiple_of(dst, TILE)
            low = pl.multiple_of(dst + edge, TILE)
            value = ref[base + row - lo : base + row - lo + size, :]
            if part == 0:
                ops_ref[pl.ds(dst, size), :occ] = value
                ops_ref[pl.ds(low, size), occ:] = value
            else:
                ops_ref[pl.ds(dst, size), occ:] = value
                ops_ref[pl.ds(low, size), :occ] = -value
            row += size

    for qq in range(nq):
        want = match_ref[qq, ka]
        for whose in range(2):
            origin = lax.bitwise_xor(ka, whose)
            origin_core = lax.bitwise_xor(core, whose)
            for part in range(2):
                pair = orders[part]
                dims = [
                    [jnp.where(origin_core == 0, pair[0][s][i], pair[1][s][i]) for i in range(2)]
                    for s in range(3)
                ]
                length = spans[part][1] - spans[part][0]
                for slot in range(8):
                    owner_ka, owner_fit = origin, fit
                    for s in range(3):
                        if slot >> s & 1:
                            owner_ka = lax.bitwise_xor(owner_ka, dims[s][0])
                            owner_fit = lax.bitwise_xor(owner_fit, dims[s][1])
                    ref = held[whose * 4 + part * 2 + slot // 4]

                    @pl.when(want == owner_ka)
                    def _():
                        place(ref, slot % 4 * length, spans[part], owner_fit)

        sums_ref[...] = jnp.zeros_like(sums_ref)
        copies[qq].wait()

        def one_block(n, c):
            rb = pl.multiple_of(lists_ref[qq, 0, 0, 0, n] * edge, edge)
            cb = pl.multiple_of(lists_ref[qq, 0, 0, 1, n] * (2 * edge), 2 * edge)
            sums_ref[pl.ds(rb, edge), :] += jnp.dot(
                l_ref[qq, n],
                ops_ref[pl.ds(cb, 2 * edge), :],
                preferred_element_type=jnp.float32,
            )
            return c

        lax.fori_loop(0, nblk, one_block, 0, unroll=16)

        def one_row(rb, c):
            x = sums_ref[pl.ds(pl.multiple_of(rb * edge, edge), edge), :].astype(jnp.bfloat16)
            x_ref[rb, :, qq * 2 * occ : (qq + 1) * 2 * occ] = x
            low = jnp.concatenate([-x[:, occ:], x[:, :occ]], axis=1)
            turned_ref[rb, qq * 2 * occ : (qq + 1) * 2 * occ, :] = jnp.concatenate([x, low], axis=0).T
            return c

        lax.fori_loop(0, nbl, one_row, 0, unroll=4)

    unit = min(edge, out_ref.shape[1])
    exchange_units(scatter_owner(False, nfit), unit, edge, x_ref, turned_ref, ex_ref, out_ref)


def rest_kernel(nfit, edge, ex_hbm, x_ref, turned_ref, out_ref, ex_ref, sem):
    copy = pltpu.make_async_copy(ex_hbm, ex_ref, sem)
    copy.start()
    copy.wait()
    unit = min(edge, out_ref.shape[1])
    exchange_units(scatter_owner(True, nfit), unit, edge, x_ref, turned_ref, ex_ref, out_ref)


def on_device(nka, nfit, integrals, block_lists, coeff, match, ex_blocks):
    nq, _, _, nblk, edge, _ = integrals.shape
    rows, occ = coeff.shape[2:]
    nexch = ex_blocks.shape[2]
    nbl = nfit * rows // edge
    held = gather_shards(coeff, nka, nfit)
    vmem = pl.BlockSpec(memory_space=pltpu.VMEM)
    hbm = pl.BlockSpec(memory_space=pltpu.HBM)
    count, chunk = nfit // 2, nexch * edge // nfit
    params = pltpu.CompilerParams(vmem_limit_bytes=28 * 1024 * 1024)
    bf16, f32, i32 = jnp.bfloat16, jnp.float32, jnp.int32
    out, xmat, turned = pl.pallas_call(
        functools.partial(half_kernel, nka, nfit, nq, nblk, edge, occ, nbl, rows),
        out_shape=[
            jax.ShapeDtypeStruct((count, chunk, 2 * edge), bf16),
            jax.ShapeDtypeStruct((nbl, edge, nq * 2 * occ), bf16),
            jax.ShapeDtypeStruct((nbl, nq * 2 * occ, 2 * edge), bf16),
        ],
        in_specs=[hbm] * 4 + [vmem] * len(held),
        out_specs=[vmem] * 3,
        scratch_shapes=[
            pltpu.SMEM(match.shape, i32),
            pltpu.SMEM(block_lists.shape, i32),
            pltpu.SMEM(ex_blocks.shape, i32),
            pltpu.VMEM((nq, nblk, edge, 2 * edge), bf16),
            pltpu.VMEM((nbl * 2 * edge, 2 * occ), bf16),
            pltpu.VMEM((nbl * edge, 2 * occ), f32),
            pltpu.SemaphoreType.DMA((nq,)),
            pltpu.SemaphoreType.DMA((3,)),
        ],
        compiler_params=params,
    )(match, block_lists, ex_blocks, integrals, *held)
    own = pl.pallas_call(
        functools.partial(rest_kernel, nfit, edge),
        out_shape=jax.ShapeDtypeStruct((count, chunk, 2 * edge), f32),
        in_specs=[hbm, vmem, vmem],
        out_specs=vmem,
        scratch_shapes=[pltpu.SMEM(ex_blocks.shape, i32), pltpu.SemaphoreType.DMA],
        compiler_params=params,
        cost_estimate=pl.CostEstimate(
            flops=nexch * edge * edge * 2 * nq * 2 * occ, bytes_accessed=1 << 23, transcendentals=0
        ),
    )(ex_blocks, xmat, turned)

    low, second = [(0, bit) for bit in bits_of(nfit)[:2]]
    total = own + swap_by(out, nka, nfit, [low, second]).astype(f32)
    steps = [[second, low]] + [[(0, bit)] * 2 for bit in bits_of(nfit)[:1:-1]]
    for by_core in steps:
        n = total.shape[0] // 2
        came = swap_by(total[n:].astype(bf16), nka, nfit, by_core)
        total = total[:n] + came.astype(f32)
    factor = -((nq * nfit * occ) ** (-0.5))
    return total * factor


def solution(mesh):
    nka, nfit = mesh.shape["ka"], mesh.shape["fit"]
    return jax.shard_map(
        functools.partial(on_device, nka, nfit),
        mesh=mesh,
        in_specs=(
            P(None, "ka", "fit", None, None, None),
            P(None, "ka", "fit", None, None),
            P("ka", None, "fit", None),
            P(),
            P("ka", None, None),
        ),
        out_specs=P("ka", "fit", None),
        check_vma=False,
    )
```

```python
import functools

import jax
import jax.numpy as jnp
from jax import lax
from jax.experimental import pallas as pl
from jax.experimental.pallas import tpu as pltpu
from jax.sharding import PartitionSpec as P

AXES = ("ka", "fit")


def bits_of(size):
    return [1 << b for b in range(size.bit_length() - 1)]


def swap_by(arr, nka, nfit, dka, dfit):
    perm = [
        (k * nfit + f, (k ^ dka) * nfit + (f ^ dfit)) for k in range(nka) for f in range(nfit)
    ]
    return lax.ppermute(arr, AXES, perm)


def far_offsets(nfit):
    offsets = [0]
    for bit in bits_of(nfit)[2:]:
        offsets = offsets + [o ^ bit for o in offsets]
    return offsets


def gather_shards(shard, nka, nfit):
    half, core = nka // 2, 1
    y, w = bits_of(nfit)[:2]
    size = shard.size // shard.shape[-1]

    def swap(arr, dka, dfit):
        return swap_by(arr, nka, nfit, dka, dfit)

    def join(*arrs):
        return jnp.concatenate(arrs, axis=0)

    own = shard.reshape(size, shard.shape[-1])
    bits = bits_of(nfit)[2:]
    near = both = own
    for bit in bits[:-1]:
        near = both = join(both, swap(both, 0, bit))
    far, x_near, y_near, xy_near = lax.optimization_barrier(
        (
            swap(near, 0, bits[-1]),
            swap(near, half, 0),
            swap(near, 0, y),
            swap(near, half, y),
        )
    )
    both = join(near, far)
    w_both, x_far, y_far, xy_far = lax.optimization_barrier(
        (swap(both, 0, w), swap(far, half, 0), swap(far, 0, y), swap(far, half, y))
    )
    xy_both = join(xy_near, xy_far)
    xw_both, yw_both, xyw_both = lax.optimization_barrier(
        (swap(w_both, half, 0), swap(w_both, 0, y), swap(xy_both, 0, w))
    )
    held = [
        ((0, 0), both),
        ((half, 0), join(x_near, x_far)),
        ((0, y), join(y_near, y_far)),
        ((half, y), xy_both),
        ((0, w), w_both),
        ((half, w), xw_both),
        ((0, y | w), yw_both),
        ((half, y | w), xyw_both),
    ]
    held = held + [((dka ^ core, dfit), swap(arr, core, 0)) for (dka, dfit), arr in held]
    return [off for off, _ in held], [arr for _, arr in held]


def exchange_units(owner_of, second, unit, edge, x_ref, turned_ref, ex_ref, out_ref):
    count, rows, _ = out_ref.shape
    for slot in range(count):
        for step in range(rows // unit):
            row = owner_of(slot) * (2 * rows) + second * rows + step * unit
            e = row // edge
            lb, rb = ex_ref[0, 0, e], ex_ref[0, 1, e]
            lo = pl.multiple_of(lax.rem(row, edge), unit)
            out_ref[slot, step * unit : (step + 1) * unit, :] = jnp.dot(
                x_ref[lb, pl.ds(lo, unit), :],
                turned_ref[rb],
                preferred_element_type=jnp.float32,
            ).astype(out_ref.dtype)


def chunk_owner(offs):
    fit = lax.axis_index("fit")
    return lambda slot: lax.bitwise_xor(fit, offs[slot])


def half_kernel(
    offsets, far, orders, nq, nblk, edge, occ, nbl, rows, match_hbm, lists_hbm, ex_hbm, lmat_ref, *refs
):
    held = refs[: len(offsets)]
    first_ref, second_ref, x_ref, turned_ref = refs[len(offsets) : len(offsets) + 4]
    match_ref, lists_ref, ex_ref, l_ref, ops_ref, sums_ref, sems, small = refs[len(offsets) + 4 :]
    ka, fit = lax.axis_index("ka"), lax.axis_index("fit")
    sub = min(rows, edge)
    loads = [
        pltpu.make_async_copy(src, dst, small.at[i])
        for i, (src, dst) in enumerate(
            [(match_hbm, match_ref), (lists_hbm, lists_ref), (ex_hbm, ex_ref)]
        )
    ]
    copies = [
        pltpu.make_async_copy(lmat_ref.at[qq, 0, 0], l_ref.at[qq], sems.at[qq]) for qq in range(nq)
    ]
    for copy in loads + copies:
        copy.start()
    for copy in loads:
        copy.wait()

    def place(ref, owner):
        for row in range(0, ref.shape[0], sub):
            piece, rest = divmod(row, 2 * rows)
            part, inner = divmod(rest, rows)
            start = lax.bitwise_xor(owner, far[piece]) * rows + inner
            dst = (start // edge) * (2 * edge) + lax.rem(start, edge)
            dst = pl.multiple_of(dst, sub)
            low = pl.multiple_of(dst + edge, sub)
            value = ref[row : row + sub, :]
            if part == 0:
                ops_ref[pl.ds(dst, sub), :occ] = value
                ops_ref[pl.ds(low, sub), occ:] = value
            else:
                ops_ref[pl.ds(dst, sub), occ:] = value
                ops_ref[pl.ds(low, sub), :occ] = -value

    for qq in range(nq):
        want = lax.bitwise_xor(match_ref[qq, ka], ka)
        for dka in sorted({off[0] for off in offsets}):

            @pl.when(want == dka)
            def _():
                for off, ref in zip(offsets, held):
                    if off[0] == dka:
                        place(ref, lax.bitwise_xor(fit, off[1]))

        sums_ref[...] = jnp.zeros_like(sums_ref)
        copies[qq].wait()

        def one_block(n, c):
            rb = pl.multiple_of(lists_ref[qq, 0, 0, 0, n] * edge, edge)
            cb = pl.multiple_of(lists_ref[qq, 0, 0, 1, n] * (2 * edge), 2 * edge)
            sums_ref[pl.ds(rb, edge), :] += jnp.dot(
                l_ref[qq, n],
                ops_ref[pl.ds(cb, 2 * edge), :],
                preferred_element_type=jnp.float32,
            )
            return c

        lax.fori_loop(0, nblk, one_block, 0, unroll=16)

        def one_row(rb, c):
            x = sums_ref[pl.ds(pl.multiple_of(rb * edge, edge), edge), :].astype(jnp.bfloat16)
            x_ref[rb, :, qq * 2 * occ : (qq + 1) * 2 * occ] = x
            low = jnp.concatenate([-x[:, occ:], x[:, :occ]], axis=1)
            turned_ref[rb, qq * 2 * occ : (qq + 1) * 2 * occ, :] = jnp.concatenate([x, low], axis=0).T
            return c

        lax.fori_loop(0, nbl, one_row, 0, unroll=4)

    unit = min(edge, first_ref.shape[1])
    for second, ref in enumerate((first_ref, second_ref)):
        exchange_units(chunk_owner(orders[second]), second, unit, edge, x_ref, turned_ref, ex_ref, ref)


def rest_kernel(orders, edge, ex_hbm, x_ref, turned_ref, first_ref, second_ref, ex_ref, sem):
    copy = pltpu.make_async_copy(ex_hbm, ex_ref, sem)
    copy.start()
    copy.wait()
    unit = min(edge, first_ref.shape[1])
    for second, ref in enumerate((first_ref, second_ref)):
        exchange_units(chunk_owner(orders[second]), second, unit, edge, x_ref, turned_ref, ex_ref, ref)


def on_device(nka, nfit, integrals, block_lists, coeff, match, ex_blocks):
    nq, _, _, nblk, edge, _ = integrals.shape
    rows, occ = coeff.shape[2:]
    nexch = ex_blocks.shape[2]
    nbl = nfit * rows // edge
    offsets, held = gather_shards(coeff, nka, nfit)
    vmem = pl.BlockSpec(memory_space=pltpu.VMEM)
    hbm = pl.BlockSpec(memory_space=pltpu.HBM)
    params = pltpu.CompilerParams(vmem_limit_bytes=28 * 1024 * 1024)
    bf16, f32, i32 = jnp.bfloat16, jnp.float32, jnp.int32

    bits, far = bits_of(nfit), far_offsets(nfit)
    y, w = bits[:2]
    keep_a = far + [o ^ w for o in far]
    keep_b = far + [o ^ y for o in far]
    send_a = [o ^ y for o in keep_a]
    send_b = [o ^ w for o in keep_b]
    count, half = nfit // 2, nexch * edge // nfit // 2
    out_a, out_b, xmat, turned = pl.pallas_call(
        functools.partial(
            half_kernel, offsets, far, (send_a, send_b), nq, nblk, edge, occ, nbl, rows
        ),
        out_shape=[jax.ShapeDtypeStruct((count, half, 2 * edge), bf16)] * 2
        + [
            jax.ShapeDtypeStruct((nbl, edge, nq * 2 * occ), bf16),
            jax.ShapeDtypeStruct((nbl, nq * 2 * occ, 2 * edge), bf16),
        ],
        in_specs=[hbm] * 4 + [vmem] * len(held),
        out_specs=[vmem] * 4,
        scratch_shapes=[
            pltpu.SMEM(match.shape, i32),
            pltpu.SMEM(block_lists.shape, i32),
            pltpu.SMEM(ex_blocks.shape, i32),
            pltpu.VMEM((nq, nblk, edge, 2 * edge), bf16),
            pltpu.VMEM((nbl * 2 * edge, 2 * occ), bf16),
            pltpu.VMEM((nbl * edge, 2 * occ), f32),
            pltpu.SemaphoreType.DMA((nq,)),
            pltpu.SemaphoreType.DMA((3,)),
        ],
        compiler_params=params,
    )(match, block_lists, ex_blocks, integrals, *held)
    own_a, own_b = pl.pallas_call(
        functools.partial(rest_kernel, (keep_a, keep_b), edge),
        out_shape=[jax.ShapeDtypeStruct((count, half, 2 * edge), f32)] * 2,
        in_specs=[hbm, vmem, vmem],
        out_specs=[vmem] * 2,
        scratch_shapes=[pltpu.SMEM(ex_blocks.shape, i32), pltpu.SemaphoreType.DMA],
        compiler_params=params,
        cost_estimate=pl.CostEstimate(
            flops=nexch * edge * edge * 2 * nq * 2 * occ, bytes_accessed=1 << 23, transcendentals=0
        ),
    )(ex_blocks, xmat, turned)

    def swap(arr, dfit):
        return swap_by(arr, nka, nfit, 0, dfit)

    n = count // 2
    sum_a = own_a + swap(out_a, y).astype(f32)
    sum_b = own_b + swap(out_b, w).astype(f32)
    got_a = swap(sum_a[n:].astype(bf16), w)
    got_b = swap(sum_b[n:].astype(bf16), y)
    total = jnp.concatenate(
        [sum_a[:n] + got_a.astype(f32), sum_b[:n] + got_b.astype(f32)], axis=1
    )
    for bit in bits[:1:-1]:
        n = n // 2
        total = total[:n] + swap(total[n:].astype(bf16), bit).astype(f32)
    factor = -((nq * nfit * occ) ** (-0.5))
    return total * factor


def solution(mesh):
    nka, nfit = mesh.shape["ka"], mesh.shape["fit"]
    return jax.shard_map(
        functools.partial(on_device, nka, nfit),
        mesh=mesh,
        in_specs=(
            P(None, "ka", "fit", None, None, None),
            P(None, "ka", "fit", None, None),
            P("ka", None, "fit", None),
            P(),
            P("ka", None, None),
        ),
        out_specs=P("ka", "fit", None),
        check_vma=False,
    )
```

```python
import functools

import jax
import jax.numpy as jnp
from jax import lax
from jax.experimental import pallas as pl
from jax.experimental.pallas import tpu as pltpu
from jax.sharding import PartitionSpec as P

AXES = ("ka", "fit")


def bits_of(size):
    return [1 << b for b in range(size.bit_length() - 1)]


def swap_by(arr, nka, nfit, dka, dfit):
    perm = [
        (k * nfit + f, (k ^ dka) * nfit + (f ^ dfit)) for k in range(nka) for f in range(nfit)
    ]
    return lax.ppermute(arr, AXES, perm)


def far_offsets(nfit):
    offsets = [0]
    for bit in bits_of(nfit)[2:]:
        offsets = offsets + [o ^ bit for o in offsets]
    return offsets


def gather_shards(shard, nka, nfit):
    half, core = nka // 2, 1
    y, w = bits_of(nfit)[:2]
    size = shard.size // shard.shape[-1]

    def swap(arr, dka, dfit):
        return swap_by(arr, nka, nfit, dka, dfit)

    def join(*arrs):
        return jnp.concatenate(arrs, axis=0)

    own = shard.reshape(size, shard.shape[-1])
    bits = bits_of(nfit)[2:]
    near = both = own
    for bit in bits[:-1]:
        near = both = join(both, swap(both, 0, bit))
    far, x_near, y_near, xy_near = lax.optimization_barrier(
        (
            swap(near, 0, bits[-1]),
            swap(near, half, 0),
            swap(near, 0, y),
            swap(near, half, y),
        )
    )
    both = join(near, far)
    w_both, x_far, y_far, xy_far = lax.optimization_barrier(
        (swap(both, 0, w), swap(far, half, 0), swap(far, 0, y), swap(far, half, y))
    )
    xy_both = join(xy_near, xy_far)
    xw_both, yw_both, xyw_both = lax.optimization_barrier(
        (swap(w_both, half, 0), swap(w_both, 0, y), swap(xy_both, 0, w))
    )
    held = [
        ((0, 0), both),
        ((half, 0), join(x_near, x_far)),
        ((0, y), join(y_near, y_far)),
        ((half, y), xy_both),
        ((0, w), w_both),
        ((half, w), xw_both),
        ((0, y | w), yw_both),
        ((half, y | w), xyw_both),
    ]
    held = held + [((dka ^ core, dfit), swap(arr, core, 0)) for (dka, dfit), arr in held]
    return [off for off, _ in held], [arr for _, arr in held]


def exchange_units(owner_of, unit, edge, x_ref, turned_ref, ex_ref, out_ref):
    count, rows, _ = out_ref.shape
    for slot in range(count):
        for step in range(rows // unit):
            row = owner_of(slot) * rows + step * unit
            e = row // edge
            lb, rb = ex_ref[0, 0, e], ex_ref[0, 1, e]
            lo = pl.multiple_of(lax.rem(row, edge), unit)
            out_ref[slot, step * unit : (step + 1) * unit, :] = jnp.dot(
                x_ref[lb, pl.ds(lo, unit), :],
                turned_ref[rb],
                preferred_element_type=jnp.float32,
            ).astype(out_ref.dtype)


def chunk_owner(offs):
    fit = lax.axis_index("fit")
    return lambda slot: lax.bitwise_xor(fit, offs[slot])


def half_kernel(
    offsets, far, orders, nq, nblk, edge, occ, nbl, rows, match_hbm, lists_hbm, ex_hbm, lmat_ref, *refs
):
    held = refs[: len(offsets)]
    outs, refs = refs[len(offsets) :][: len(orders)], refs[len(offsets) + len(orders) :]
    x_ref, turned_ref, match_ref, lists_ref, ex_ref, l_ref, ops_ref, sums_ref, sems, small = refs
    ka, fit = lax.axis_index("ka"), lax.axis_index("fit")
    sub = min(rows, edge)
    loads = [
        pltpu.make_async_copy(src, dst, small.at[i])
        for i, (src, dst) in enumerate(
            [(match_hbm, match_ref), (lists_hbm, lists_ref), (ex_hbm, ex_ref)]
        )
    ]
    copies = [
        pltpu.make_async_copy(lmat_ref.at[qq, 0, 0], l_ref.at[qq], sems.at[qq]) for qq in range(nq)
    ]
    for copy in loads + copies:
        copy.start()
    for copy in loads:
        copy.wait()

    def place(ref, owner):
        for row in range(0, ref.shape[0], sub):
            piece, rest = divmod(row, 2 * rows)
            part, inner = divmod(rest, rows)
            start = lax.bitwise_xor(owner, far[piece]) * rows + inner
            dst = (start // edge) * (2 * edge) + lax.rem(start, edge)
            dst = pl.multiple_of(dst, sub)
            low = pl.multiple_of(dst + edge, sub)
            value = ref[row : row + sub, :]
            if part == 0:
                ops_ref[pl.ds(dst, sub), :occ] = value
                ops_ref[pl.ds(low, sub), occ:] = value
            else:
                ops_ref[pl.ds(dst, sub), occ:] = value
                ops_ref[pl.ds(low, sub), :occ] = -value

    for qq in range(nq):
        want = lax.bitwise_xor(match_ref[qq, ka], ka)
        for dka in sorted({off[0] for off in offsets}):

            @pl.when(want == dka)
            def _():
                for off, ref in zip(offsets, held):
                    if off[0] == dka:
                        place(ref, lax.bitwise_xor(fit, off[1]))

        sums_ref[...] = jnp.zeros_like(sums_ref)
        copies[qq].wait()

        def one_block(n, c):
            rb = pl.multiple_of(lists_ref[qq, 0, 0, 0, n] * edge, edge)
            cb = pl.multiple_of(lists_ref[qq, 0, 0, 1, n] * (2 * edge), 2 * edge)
            sums_ref[pl.ds(rb, edge), :] += jnp.dot(
                l_ref[qq, n],
                ops_ref[pl.ds(cb, 2 * edge), :],
                preferred_element_type=jnp.float32,
            )
            return c

        lax.fori_loop(0, nblk, one_block, 0, unroll=True)

        def one_row(rb, c):
            x = sums_ref[pl.ds(pl.multiple_of(rb * edge, edge), edge), :].astype(jnp.bfloat16)
            x_ref[rb, :, qq * 2 * occ : (qq + 1) * 2 * occ] = x
            low = jnp.concatenate([-x[:, occ:], x[:, :occ]], axis=1)
            turned_ref[rb, qq * 2 * occ : (qq + 1) * 2 * occ, :] = jnp.concatenate([x, low], axis=0).T
            return c

        lax.fori_loop(0, nbl, one_row, 0, unroll=True)

    unit = min(edge, outs[0].shape[1])
    for order, ref in zip(orders, outs):
        exchange_units(chunk_owner(order), unit, edge, x_ref, turned_ref, ex_ref, ref)


def rest_kernel(orders, edge, ex_hbm, x_ref, turned_ref, *refs):
    outs, (ex_ref, sem) = refs[: len(orders)], refs[len(orders) :]
    copy = pltpu.make_async_copy(ex_hbm, ex_ref, sem)
    copy.start()
    copy.wait()
    unit = min(edge, outs[0].shape[1])
    for order, ref in zip(orders, outs):
        exchange_units(chunk_owner(order), unit, edge, x_ref, turned_ref, ex_ref, ref)


def on_device(nka, nfit, integrals, block_lists, coeff, match, ex_blocks):
    nq, _, _, nblk, edge, _ = integrals.shape
    rows, occ = coeff.shape[2:]
    nexch = ex_blocks.shape[2]
    nbl = nfit * rows // edge
    offsets, held = gather_shards(coeff, nka, nfit)

    def in_hbm(arr):
        return pltpu.with_memory_space_constraint(arr, pltpu.HBM)

    tables = [in_hbm(arr) for arr in (match, block_lists, ex_blocks)]
    vmem = pl.BlockSpec(memory_space=pltpu.VMEM)
    hbm = pl.BlockSpec(memory_space=pltpu.HBM)
    params = pltpu.CompilerParams(vmem_limit_bytes=28 * 1024 * 1024)
    bf16, f32, i32 = jnp.bfloat16, jnp.float32, jnp.int32

    bits, far = bits_of(nfit), far_offsets(nfit)
    y, w = bits[:2]
    near = (y, w, y | w)
    far_sends = [[o ^ n for o in far[1:]] for n in near]
    near_sends = [[n] for n in near]
    chunk = nexch * edge // nfit

    def chunks(orders, dtypes):
        return [
            jax.ShapeDtypeStruct((len(order), chunk, 2 * edge), dtype)
            for order, dtype in zip(orders, dtypes)
        ]

    *far_out, xmat, turned = pl.pallas_call(
        functools.partial(
            half_kernel, offsets, far, far_sends, nq, nblk, edge, occ, nbl, rows
        ),
        out_shape=chunks(far_sends, [bf16] * 3)
        + [
            jax.ShapeDtypeStruct((nbl, edge, nq * 2 * occ), bf16),
            jax.ShapeDtypeStruct((nbl, nq * 2 * occ, 2 * edge), bf16),
        ],
        in_specs=[hbm] * 4 + [vmem] * len(held),
        out_specs=[vmem] * 5,
        scratch_shapes=[
            pltpu.SMEM(match.shape, i32),
            pltpu.SMEM(block_lists.shape, i32),
            pltpu.SMEM(ex_blocks.shape, i32),
            pltpu.VMEM((nq, nblk, edge, 2 * edge), bf16),
            pltpu.VMEM((nbl * 2 * edge, 2 * occ), bf16),
            pltpu.VMEM((nbl * edge, 2 * occ), f32),
            pltpu.SemaphoreType.DMA((nq,)),
            pltpu.SemaphoreType.DMA((3,)),
        ],
        compiler_params=params,
    )(*tables, in_hbm(integrals), *held)

    def rest(orders, dtypes):
        return pl.pallas_call(
            functools.partial(rest_kernel, orders, edge),
            out_shape=chunks(orders, dtypes),
            in_specs=[hbm, vmem, vmem],
            out_specs=[vmem] * len(orders),
            scratch_shapes=[pltpu.SMEM(ex_blocks.shape, i32), pltpu.SemaphoreType.DMA],
            compiler_params=params,
            cost_estimate=pl.CostEstimate(
                flops=nexch * edge * edge * 2 * nq * 2 * occ, bytes_accessed=1 << 23, transcendentals=0
            ),
        )(tables[2], xmat, turned)

    def swap(arr, dfit):
        return swap_by(arr, nka, nfit, 0, dfit)

    *near_out, own = rest(near_sends + [far], [bf16] * 3 + [f32])
    far_got = [swap(arr, n).astype(f32) for arr, n in zip(far_out, near)]
    near_got = [swap(arr, n).astype(f32) for arr, n in zip(near_out, near)]
    parts = own[1:] + far_got[0] + far_got[1] + far_got[2]
    home = own[:1]
    size = len(far)
    for bit in bits[:1:-1]:
        size = size // 2
        came = swap(parts[size - 1 :].astype(bf16), bit).astype(f32)
        home = home + came[:1]
        if size > 1:
            parts = parts[: size - 1] + came[1:]
    home = home + near_got[0] + near_got[1] + near_got[2]
    factor = -((nq * nfit * occ) ** (-0.5))
    return home * factor


def solution(mesh):
    nka, nfit = mesh.shape["ka"], mesh.shape["fit"]
    return jax.shard_map(
        functools.partial(on_device, nka, nfit),
        mesh=mesh,
        in_specs=(
            P(None, "ka", "fit", None, None, None),
            P(None, "ka", "fit", None, None),
            P("ka", None, "fit", None),
            P(),
            P("ka", None, None),
        ),
        out_specs=P("ka", "fit", None),
        check_vma=False,
    )
```

```python
import functools

import jax
import jax.numpy as jnp
from jax import lax
from jax.experimental import pallas as pl
from jax.experimental.pallas import tpu as pltpu
from jax.sharding import PartitionSpec as P

AXES = ("ka", "fit")


def bits_of(size):
    return [1 << b for b in range(size.bit_length() - 1)]


def swap_by(arr, nka, nfit, dka, dfit):
    perm = [
        (k * nfit + f, (k ^ dka) * nfit + (f ^ dfit)) for k in range(nka) for f in range(nfit)
    ]
    return lax.ppermute(arr, AXES, perm)


def far_offsets(nfit):
    offsets = [0]
    for bit in bits_of(nfit)[2:]:
        offsets = offsets + [o ^ bit for o in offsets]
    return offsets


def gather_shards(shard, nka, nfit):
    half, core = nka // 2, 1
    y, w = bits_of(nfit)[:2]
    size = shard.size // shard.shape[-1]

    def swap(arr, dka, dfit):
        return swap_by(arr, nka, nfit, dka, dfit)

    def join(*arrs):
        return jnp.concatenate(arrs, axis=0)

    own = shard.reshape(size, shard.shape[-1])
    bits = bits_of(nfit)[2:]
    near = both = own
    for bit in bits[:-1]:
        near = both = join(both, swap(both, 0, bit))
    room = join(near, jnp.zeros_like(near))
    room, far, x_near, y_near, xy_near = lax.optimization_barrier(
        (
            room,
            swap(near, 0, bits[-1]),
            swap(near, half, 0),
            swap(near, 0, y),
            swap(near, half, y),
        )
    )
    both = lax.dynamic_update_slice(room, far, (near.shape[0], 0))
    w_both, x_far, y_far, xy_far = lax.optimization_barrier(
        (swap(both, 0, w), swap(far, half, 0), swap(far, 0, y), swap(far, half, y))
    )
    xy_both = join(xy_near, xy_far)
    xw_both, yw_both, xyw_both = lax.optimization_barrier(
        (swap(w_both, half, 0), swap(w_both, 0, y), swap(xy_both, 0, w))
    )
    held = [
        ((0, 0), both),
        ((half, 0), join(x_near, x_far)),
        ((0, y), join(y_near, y_far)),
        ((half, y), xy_both),
        ((0, w), w_both),
        ((half, w), xw_both),
        ((0, y | w), yw_both),
        ((half, y | w), xyw_both),
    ]
    held = held + [((dka ^ core, dfit), swap(arr, core, 0)) for (dka, dfit), arr in held]
    return [off for off, _ in held], [arr for _, arr in held]


def exchange_units(owner_of, unit, edge, x_ref, turned_ref, ex_ref, out_ref):
    count, rows, _ = out_ref.shape
    for slot in range(count):
        for step in range(rows // unit):
            row = owner_of(slot) * rows + step * unit
            e = row // edge
            lb, rb = ex_ref[0, 0, e], ex_ref[0, 1, e]
            lo = pl.multiple_of(lax.rem(row, edge), unit)
            out_ref[slot, step * unit : (step + 1) * unit, :] = jnp.dot(
                x_ref[lb, pl.ds(lo, unit), :],
                turned_ref[rb],
                preferred_element_type=jnp.float32,
            ).astype(out_ref.dtype)


def chunk_owner(offs):
    fit = lax.axis_index("fit")
    return lambda slot: lax.bitwise_xor(fit, offs[slot])


def half_kernel(
    offsets, far, orders, nq, nblk, edge, occ, nbl, rows, match_hbm, lists_hbm, ex_hbm, lmat_ref, *refs
):
    held = refs[: len(offsets)]
    outs, refs = refs[len(offsets) :][: len(orders)], refs[len(offsets) + len(orders) :]
    x_ref, turned_ref, match_ref, lists_ref, ex_ref, l_ref, ops_ref, sums_ref, sems, small = refs
    ka, fit = lax.axis_index("ka"), lax.axis_index("fit")
    sub = min(rows, edge)
    loads = [
        pltpu.make_async_copy(src, dst, small.at[i])
        for i, (src, dst) in enumerate(
            [(match_hbm, match_ref), (lists_hbm, lists_ref), (ex_hbm, ex_ref)]
        )
    ]
    copies = [
        pltpu.make_async_copy(lmat_ref.at[qq, 0, 0], l_ref.at[qq], sems.at[qq]) for qq in range(nq)
    ]
    for copy in loads + copies:
        copy.start()
    for copy in loads:
        copy.wait()

    def place(ref, owner):
        for row in range(0, ref.shape[0], sub):
            piece, rest = divmod(row, 2 * rows)
            part, inner = divmod(rest, rows)
            start = lax.bitwise_xor(owner, far[piece]) * rows + inner
            dst = (start // edge) * (2 * edge) + lax.rem(start, edge)
            dst = pl.multiple_of(dst, sub)
            low = pl.multiple_of(dst + edge, sub)
            value = ref[row : row + sub, :]
            if part == 0:
                ops_ref[pl.ds(dst, sub), :occ] = value
                ops_ref[pl.ds(low, sub), occ:] = value
            else:
                ops_ref[pl.ds(dst, sub), occ:] = value
                ops_ref[pl.ds(low, sub), :occ] = -value

    for qq in range(nq):
        want = lax.bitwise_xor(match_ref[qq, ka], ka)
        for dka in sorted({off[0] for off in offsets}):

            @pl.when(want == dka)
            def _():
                for off, ref in zip(offsets, held):
                    if off[0] == dka:
                        place(ref, lax.bitwise_xor(fit, off[1]))

        sums_ref[...] = jnp.zeros_like(sums_ref)
        copies[qq].wait()

        def one_block(n, c):
            rb = pl.multiple_of(lists_ref[qq, 0, 0, 0, n] * edge, edge)
            cb = pl.multiple_of(lists_ref[qq, 0, 0, 1, n] * (2 * edge), 2 * edge)
            sums_ref[pl.ds(rb, edge), :] += jnp.dot(
                l_ref[qq, n],
                ops_ref[pl.ds(cb, 2 * edge), :],
                preferred_element_type=jnp.float32,
            )
            return c

        lax.fori_loop(0, nblk, one_block, 0, unroll=True)

        def one_row(rb, c):
            x = sums_ref[pl.ds(pl.multiple_of(rb * edge, edge), edge), :].astype(jnp.bfloat16)
            x_ref[rb, :, qq * 2 * occ : (qq + 1) * 2 * occ] = x
            low = jnp.concatenate([-x[:, occ:], x[:, :occ]], axis=1)
            turned_ref[rb, qq * 2 * occ : (qq + 1) * 2 * occ, :] = jnp.concatenate([x, low], axis=0).T
            return c

        lax.fori_loop(0, nbl, one_row, 0, unroll=True)

    unit = min(edge, outs[0].shape[1])
    for order, ref in zip(orders, outs):
        exchange_units(chunk_owner(order), unit, edge, x_ref, turned_ref, ex_ref, ref)


def rest_kernel(orders, edge, ex_hbm, x_ref, turned_ref, *refs):
    outs, (ex_ref, sem) = refs[: len(orders)], refs[len(orders) :]
    copy = pltpu.make_async_copy(ex_hbm, ex_ref, sem)
    copy.start()
    copy.wait()
    unit = min(edge, outs[0].shape[1])
    for order, ref in zip(orders, outs):
        exchange_units(chunk_owner(order), unit, edge, x_ref, turned_ref, ex_ref, ref)


def on_device(nka, nfit, integrals, block_lists, coeff, match, ex_blocks):
    nq, _, _, nblk, edge, _ = integrals.shape
    rows, occ = coeff.shape[2:]
    nexch = ex_blocks.shape[2]
    nbl = nfit * rows // edge
    offsets, held = gather_shards(coeff, nka, nfit)

    def in_hbm(arr):
        return pltpu.with_memory_space_constraint(arr, pltpu.HBM)

    tables = [in_hbm(arr) for arr in (match, block_lists, ex_blocks)]
    vmem = pl.BlockSpec(memory_space=pltpu.VMEM)
    hbm = pl.BlockSpec(memory_space=pltpu.HBM)
    params = pltpu.CompilerParams(vmem_limit_bytes=28 * 1024 * 1024)
    bf16, f32, i32 = jnp.bfloat16, jnp.float32, jnp.int32

    bits, far = bits_of(nfit), far_offsets(nfit)
    y, w = bits[:2]
    near = (y, w, y | w)
    far_sends = [[o ^ n for o in far[1:]] for n in near]
    near_sends = [[n] for n in near]
    chunk = nexch * edge // nfit

    def chunks(orders, dtypes):
        return [
            jax.ShapeDtypeStruct((len(order), chunk, 2 * edge), dtype)
            for order, dtype in zip(orders, dtypes)
        ]

    *far_out, xmat, turned = pl.pallas_call(
        functools.partial(
            half_kernel, offsets, far, far_sends, nq, nblk, edge, occ, nbl, rows
        ),
        out_shape=chunks(far_sends, [bf16] * 3)
        + [
            jax.ShapeDtypeStruct((nbl, edge, nq * 2 * occ), bf16),
            jax.ShapeDtypeStruct((nbl, nq * 2 * occ, 2 * edge), bf16),
        ],
        in_specs=[hbm] * 4 + [vmem] * len(held),
        out_specs=[vmem] * 5,
        scratch_shapes=[
            pltpu.SMEM(match.shape, i32),
            pltpu.SMEM(block_lists.shape, i32),
            pltpu.SMEM(ex_blocks.shape, i32),
            pltpu.VMEM((nq, nblk, edge, 2 * edge), bf16),
            pltpu.VMEM((nbl * 2 * edge, 2 * occ), bf16),
            pltpu.VMEM((nbl * edge, 2 * occ), f32),
            pltpu.SemaphoreType.DMA((nq,)),
            pltpu.SemaphoreType.DMA((3,)),
        ],
        compiler_params=params,
    )(*tables, in_hbm(integrals), *held)

    def rest(orders, dtypes):
        return pl.pallas_call(
            functools.partial(rest_kernel, orders, edge),
            out_shape=chunks(orders, dtypes),
            in_specs=[hbm, vmem, vmem],
            out_specs=[vmem] * len(orders),
            scratch_shapes=[pltpu.SMEM(ex_blocks.shape, i32), pltpu.SemaphoreType.DMA],
            compiler_params=params,
            cost_estimate=pl.CostEstimate(
                flops=nexch * edge * edge * 2 * nq * 2 * occ, bytes_accessed=1 << 23, transcendentals=0
            ),
        )(tables[2], xmat, turned)

    def swap(arr, dfit):
        return swap_by(arr, nka, nfit, 0, dfit)

    *near_out, own = rest(near_sends + [far], [bf16] * 3 + [f32])
    far_got = [swap(arr, n).astype(f32) for arr, n in zip(far_out, near)]
    near_got = [swap(arr, n).astype(f32) for arr, n in zip(near_out, near)]
    parts = own[1:] + far_got[0] + far_got[1] + far_got[2]
    home = own[:1]
    size = len(far)
    for bit in bits[:1:-1]:
        size = size // 2
        came = swap(parts[size - 1 :].astype(bf16), bit).astype(f32)
        home = home + came[:1]
        if size > 1:
            parts = parts[: size - 1] + came[1:]
    home = home + near_got[0] + near_got[1] + near_got[2]
    factor = -((nq * nfit * occ) ** (-0.5))
    return home * factor


def solution(mesh):
    nka, nfit = mesh.shape["ka"], mesh.shape["fit"]
    return jax.shard_map(
        functools.partial(on_device, nka, nfit),
        mesh=mesh,
        in_specs=(
            P(None, "ka", "fit", None, None, None),
            P(None, "ka", "fit", None, None),
            P("ka", None, "fit", None),
            P(),
            P("ka", None, None),
        ),
        out_specs=P("ka", "fit", None),
        check_vma=False,
    )
```
